256 devices in a mesh: grp: 16 (over y, x_hi, core), leaf: 16 (over x_lo, z).
Axes of the slice: x: 4 (x_hi: 2, x_lo: 2; x = x_hi * 2 + x_lo), y: 4, z: 8, core: 2. Of those that a mesh axis runs over, the one named last changes fastest.
Arguments:
- labels: int32 [131072], P(('grp', 'leaf')), may hold values from 0 to 255
- leaf_inverse: float32 [131072, 512], P(('grp', 'leaf')), may hold values from -1 to 4
- leaf_basis: float32 [131072, 128], P(('grp', 'leaf')), may hold values from -0.25 to 0.25
- leaf_solved: float32 [131072, 128], P(('grp', 'leaf')), may hold values from -0.5 to 0.5
- group_capacitance: float32 [32768, 2048], P(('grp', 'leaf')), may hold values from -1 to 4
- top_basis: float32 [131072, 128], P(('grp', 'leaf')), may hold values from -0.0625 to 0.0625
- top_solved: float32 [131072, 128], P(('grp', 'leaf')), may hold values from -0.5 to 0.5
- top_capacitance: float32 [2048, 2048], P('grp'), may hold values from -1 to 4
Outputs:
- dual_box: float32 [131072, 256], P(('grp', 'leaf'))
- scaled_dual: float32 [131072, 256], P(('grp', 'leaf'))
The draws below stay inside these ranges and needn't reach their ends.
All inputs are finite; a program needn't handle non-finite values.
Results may differ from the reference program's by a relative error of at most 0.0003.
Values sent between devices are 32-bit elements; how exact they have to be, the bound alone decides.
No kernel may reach another device: no remote copies, remote signals or barrier semaphores. Data moves between devices by JAX's collectives and lax.ppermute only.
A program may use at most 64 MiB of HBM per device.

```python
import math
import jax
import jax.numpy as jnp
from jax import lax

LEAF = 512
RANK = 128
CLASSES = 256
ITERS = 2
CAP = 2048
TOPCAP = 2048
ROWS = 131072
N_GRP = 16
N_LEAF = 16


def dominant(key, height, order):
    first, second = jax.random.split(key, 2)
    noise = jnp.clip(jax.random.normal(first, (height, order), jnp.float32), -4.0, 4.0) * 0.4
    noise = noise / math.sqrt(order)
    diagonal = jax.random.uniform(second, (height, 1), jnp.float32, 0.5, 1.5)
    position = lax.broadcasted_iota(jnp.int32, (height, order), 0) % order
    column = lax.broadcasted_iota(jnp.int32, (height, order), 1)
    identity = (position == column).astype(jnp.float32)
    return identity * diagonal + noise


def draw_leaf_inverse(key, part):
    return dominant(jax.random.fold_in(key, 11), ROWS, LEAF)


def draw_group_capacitance(key, part):
    return dominant(jax.random.fold_in(key, 23), N_GRP * CAP, CAP)


def draw_top_capacitance(key, part):
    return dominant(jax.random.fold_in(key, 37), TOPCAP, TOPCAP)


def place_ends(array, own_key, smallest, top_value):
    shape = array.shape
    place = [jax.random.randint(jax.random.fold_in(own_key, axis), (), 0, shape[axis]) for axis in range(len(shape))]
    array = array.at[tuple(place)].set(smallest)
    longest = shape.index(max(shape))
    place[longest] = (place[longest] + 1) % shape[longest]
    return array.at[tuple(place)].set(top_value)


def block_scale(rng, shape, cuts, low, top_value):
    def one(axis_at, shards_of):
        draws = jax.random.uniform(jax.random.fold_in(jax.random.fold_in(rng, 6), axis_at), (shards_of,), jnp.float32, low / len(cuts), top_value / len(cuts))
        return jnp.repeat(jnp.exp(draws), shape[axis_at] // shards_of).reshape((-1,) + (1,) * (len(shape) - axis_at - 1))

    factor_of = one(*cuts[0])
    for cut in cuts[1:]:
        factor_of = factor_of * one(*cut)
    return factor_of


def normal_values(key, shape, scale, most, cuts=(), dtype=jnp.bfloat16):
    factor_of = block_scale(key, shape, cuts, -0.22, 0.18) if cuts else 1.0
    result = jax.random.normal(key, shape, jnp.float32) * scale * factor_of
    return jnp.minimum(jnp.maximum(result, -most), most).astype(dtype)


def setup_inputs(seed: int = 0) -> dict:
    keys = jax.random.split(jax.random.key(seed), 9)
    return {
        "labels": place_ends(jax.random.randint(keys[0], (ROWS,), 0, CLASSES), jax.random.fold_in(keys[0], 1), 0, CLASSES - 1).astype(jnp.int32),
        "leaf_inverse": draw_leaf_inverse(jax.random.fold_in(keys[8], 71), 0),
        "leaf_basis": normal_values(keys[2], (ROWS, RANK), LEAF ** -0.5, 0.25, ((0, 256),), jnp.float32),
        "leaf_solved": normal_values(keys[3], (ROWS, RANK), RANK ** -0.5, 0.5, ((0, 256),), jnp.float32),
        "group_capacitance": draw_group_capacitance(jax.random.fold_in(keys[8], 71), 0),
        "top_basis": normal_values(keys[5], (ROWS, RANK), (LEAF * N_LEAF) ** -0.5, 0.0625, ((0, 256),), jnp.float32),
        "top_solved": normal_values(keys[6], (ROWS, RANK), RANK ** -0.5, 0.5, ((0, 256),), jnp.float32),
        "top_capacitance": draw_top_capacitance(jax.random.fold_in(keys[8], 71), 0),
    }


high = lax.Precision.HIGHEST


def reference(labels, leaf_inverse, leaf_basis, leaf_solved, group_capacitance, top_basis, top_solved, top_capacitance):
    leaves = N_GRP * N_LEAF
    columns = lax.broadcasted_iota(jnp.int32, (ROWS, CLASSES), 1)
    label_sign = jnp.where(labels[:, None] == columns, 1.0, -1.0).astype(jnp.float32)
    blocks = leaf_inverse.reshape(leaves, LEAF, LEAF)
    basis = leaf_basis.reshape(leaves, LEAF, RANK)
    solved_basis = leaf_solved.reshape(leaves, LEAF, RANK)
    group_blocks = group_capacitance.reshape(N_GRP, CAP, CAP)
    top_rows = top_basis.reshape(leaves, LEAF, RANK)
    top_lift = top_solved.reshape(N_GRP, N_LEAF, LEAF, RANK)
    dual_box = jnp.zeros((ROWS, CLASSES), jnp.float32)
    scaled_dual = jnp.zeros((ROWS, CLASSES), jnp.float32)
    for iteration in range(ITERS):
        rhs = label_sign * (1.0 + 1.0 * (dual_box - scaled_dual))
        local = jnp.einsum("nij,njc->nic", blocks, rhs.reshape(leaves, LEAF, CLASSES), precision=high)
        coeffs = jnp.einsum("nir,nic->nrc", basis, local, precision=high).reshape(N_GRP, CAP, CLASSES)
        group_coef = jnp.einsum("gij,gjc->gic", group_blocks, coeffs, precision=high).reshape(leaves, RANK, CLASSES)
        inner = local - jnp.einsum("nir,nrc->nic", solved_basis, group_coef, precision=high)
        projection = jnp.einsum("nir,nic->nrc", top_rows, inner, precision=high)
        projection = projection.reshape(N_GRP, N_LEAF, RANK, CLASSES).sum(axis=1).reshape(TOPCAP, CLASSES)
        top_coef = jnp.dot(top_capacitance, projection, precision=high).reshape(N_GRP, RANK, CLASSES)
        solved = inner.reshape(N_GRP, N_LEAF, LEAF, CLASSES) - jnp.einsum("glir,grc->glic", top_lift, top_coef, precision=high)
        moved = scaled_dual + label_sign * solved.reshape(ROWS, CLASSES)
        dual_box = jnp.clip(moved, 0.0, 1.0)
        scaled_dual = moved - dual_box
    return dual_box, scaled_dual
```

```python
import jax
import jax.numpy as jnp
from jax import lax
from jax.sharding import PartitionSpec as P

CLASSES = 256
ITERS = 2
RANK = 128

SQUARES = [[0, 1, 8, 9], [2, 3, 10, 11], [4, 5, 12, 13], [6, 7, 14, 15]]
STRIDES = [[0, 2, 4, 6], [1, 3, 5, 7], [8, 10, 12, 14], [9, 11, 13, 15]]


def dot(left, right, left_dim, right_dim):
    return lax.dot_general(
        left,
        right,
        (((left_dim,), (right_dim,)), ((), ())),
        precision=lax.Precision.HIGH,
        preferred_element_type=jnp.float32,
    )


def from_everyone(shard, axis):
    devices = lax.axis_size(axis)
    return lax.all_to_all(
        jnp.broadcast_to(shard[None], (devices, *shard.shape)), axis, 0, 0, tiled=True
    )


def in_place(blocks, positions):
    height = blocks[0].shape[0]
    stack = jnp.zeros((height * len(blocks), *blocks[0].shape[1:]), blocks[0].dtype)
    for block, position in zip(blocks, positions):
        stack = lax.dynamic_update_slice(stack, block, (position * height, 0))
    return stack


def across_square(pieces):
    moved = [pieces[0]]
    for q in range(1, 4):
        away = (q // 2) * 8 + q % 2
        moved.append(lax.ppermute(pieces[q], "leaf", [(i, i ^ away) for i in range(16)]))
    return moved


def along_stride(block):
    found = [block]
    for k in range(1, 4):
        pairs = [(i, (i // 8) * 8 + (i % 8 - 2 * k) % 8) for i in range(16)]
        found.append(lax.ppermute(block, "leaf", pairs))
    return found


def shards(
    labels,
    leaf_inverse,
    leaf_basis,
    leaf_solved,
    group_capacitance,
    top_basis,
    top_solved,
    top_capacitance,
):
    leaf = lax.axis_index("leaf")
    x, z = leaf // 8, leaf % 8
    parity, step = z % 2, z // 2
    place = x * 2 + parity

    lifted = dot(leaf_solved, top_basis, 0, 0)
    pieces = []
    for q in range(4):
        first = (x ^ (q // 2)) * 8 + (parity ^ (q % 2))
        columns = [
            lax.dynamic_slice(group_capacitance, (0, (first + 2 * j) * RANK), (RANK, RANK))
            for j in range(4)
        ]
        pieces.append(jnp.concatenate(columns + [lifted], axis=1))
    square = in_place(across_square(pieces), [place ^ q for q in range(4)])
    block, lifts = square[:, : 4 * RANK], square[:, 4 * RANK :]

    columns = lax.broadcasted_iota(jnp.int32, (labels.shape[0], CLASSES), 1)
    label_sign = jnp.where(labels[:, None] == columns, 1.0, -1.0).astype(jnp.float32)
    dual_box = jnp.zeros((labels.shape[0], CLASSES), jnp.float32)
    scaled_dual = jnp.zeros((labels.shape[0], CLASSES), jnp.float32)
    for iteration in range(ITERS):
        rhs = label_sign * (1.0 + 1.0 * (dual_box - scaled_dual))
        local = dot(leaf_inverse, rhs, 1, 0)
        coeffs = dot(leaf_basis, local, 0, 0)
        stacked = in_place(along_stride(coeffs), [(step + k) % 4 for k in range(4)])
        partial_coef = dot(block, stacked, 1, 0)
        group_coef = lax.psum_scatter(
            partial_coef, "leaf", scatter_dimension=0, axis_index_groups=SQUARES, tiled=True
        )
        partial_proj = dot(local, top_basis, 0, 0) - dot(partial_coef, lifts, 0, 0)
        tiles = lax.all_to_all(partial_proj.reshape(16, 16, RANK), "leaf", 0, 0, tiled=True)
        share = jnp.sum(tiles, axis=0)
        gathered = from_everyone(share, "grp")
        wide = jnp.moveaxis(gathered, 0, 1).reshape(16, 16 * RANK)
        share_coef = dot(wide, top_capacitance, 1, 1)
        top_coef = from_everyone(share_coef, "leaf").reshape(CLASSES, RANK)
        inner = local - dot(leaf_solved, group_coef, 1, 0)
        solved = inner - dot(top_solved, top_coef, 1, 1)
        moved = scaled_dual + label_sign * solved
        dual_box = jnp.clip(moved, 0.0, 1.0)
        scaled_dual = moved - dual_box
    return (dual_box, scaled_dual)


def solution(mesh):
    split = P(("grp", "leaf"), None)
    return jax.shard_map(
        shards,
        mesh=mesh,
        in_specs=(P(("grp", "leaf")), split, split, split, split, split, split, P("grp", None)),
        out_specs=(split, split),
        check_vma=False,
    )
```

```python
import functools

import jax
import jax.numpy as jnp
from jax import lax
from jax.experimental import pallas as pl
from jax.experimental.pallas import tpu as pltpu
from jax.sharding import PartitionSpec as P

CLASSES = 256
RANK = 128
LEAF = 512
BOTH = ("grp", "leaf")


def partner(core, z):
    return (((z + core) ^ 1) - core) % 8


def devices():
    return [(g, i // 8, i % 8) for g in range(16) for i in range(16)]


def index(g, x, z):
    return g * 16 + x * 8 + z


def square_pairs(q):
    pairs = []
    for g, x, z in devices():
        other = index(g, x ^ (q // 2), partner(g % 2, z) if q % 2 else z)
        pairs.append((index(g, x, z), other))
    return pairs


def stride_pairs(k):
    return [(index(g, x, z), index(g, x, (z - 2 * k) % 8)) for g, x, z in devices()]


def square_groups():
    groups = []
    for g in range(16):
        for low in range(g % 2, 8, 2):
            high = (low + 1) % 8
            groups.append([index(g, x, z) for x in range(2) for z in (low, high)])
    return groups


def stride_groups():
    return [
        [index(g, x, parity + 2 * j) for j in range(4)]
        for g in range(16)
        for x in range(2)
        for parity in range(2)
    ]


def split(value):
    high = value.astype(jnp.bfloat16)
    return high, (value - high.astype(jnp.float32)).astype(jnp.bfloat16)


def passes(left, right, right_dim=0):
    def one(a, b):
        return lax.dot_general(
            a, b, (((1,), (right_dim,)), ((), ())), preferred_element_type=jnp.float32
        )

    total = one(left[1], right[0])
    if right[1] is not None:
        total = total + one(left[0], right[1])
    return total + one(left[0], right[0])


def times(left, right, right_dim=0):
    return passes(split(left), split(right), right_dim)


def signs(labels):
    spread = jnp.broadcast_to(labels.astype(jnp.float32), (RANK, LEAF)).T
    lane = lax.broadcasted_iota(jnp.int32, (LEAF, RANK), 1).astype(jnp.float32)
    halves = [jnp.where(spread == lane + RANK * h, 1.0, -1.0) for h in range(2)]
    return jnp.concatenate(halves, axis=1).astype(jnp.float32)


def as_tiles(projection):
    return projection.T.reshape(16, 16, RANK)


def place_of():
    leaf, core = lax.axis_index("leaf"), lax.axis_index("grp") % 2
    x, z = leaf // 8, leaf % 8
    return x, z, (z + core) % 2


def cut_kernel(capacitance, solved, basis, *pieces):
    x, z, _ = place_of()
    lifted = times(solved[...].T, basis[...])
    for q in range(4):
        first = ((x + q // 2) % 2) * 8 + (z + q) % 2
        for j in range(4):
            start = pl.multiple_of((first + 2 * j) * RANK, RANK)
            pieces[q][:, j * RANK : (j + 1) * RANK] = capacitance[:, pl.ds(start, RANK)]
        pieces[q][:, 4 * RANK :] = lifted


def first_kernel(labels, inverse, basis, top, local, coeffs, projection):
    sign = signs(labels[...])
    found = passes(split(inverse[...]), (sign.astype(jnp.bfloat16), None))
    local[...] = found
    parts = split(found)
    coeffs[...] = passes(split(basis[...].T), parts)
    projection[...] = passes(split(top[...].T), parts)


def stack_coeffs(pieces, stacked):
    step = (lax.axis_index("leaf") % 8) // 2
    for k in range(4):
        start = pl.multiple_of(((step + k) % 4) * RANK, RANK)
        stacked[pl.ds(start, RANK), :] = pieces[k][...]


def row_start(q):
    x, _, low = place_of()
    return pl.multiple_of((((x + q // 2) % 2) * 2 + (low + q) % 2) * RANK, RANK)


def group_kernel(*refs):
    blocks, pieces, (projection, partial, tiles, stacked) = refs[:4], refs[4:8], refs[8:]
    stack_coeffs(pieces, stacked)
    right = split(stacked[...])
    total = projection[...]
    for q in range(4):
        rows = passes(split(blocks[q][:, : 4 * RANK]), right)
        partial[pl.ds(row_start(q), RANK), :] = rows
        total = total - times(blocks[q][:, 4 * RANK :].T, rows)
    tiles[...] = as_tiles(total)


def later_group_kernel(*refs):
    blocks, pieces, (partial, stacked) = refs[:4], refs[4:8], refs[8:]
    stack_coeffs(pieces, stacked)
    right = split(stacked[...])
    for q in range(4):
        partial[pl.ds(row_start(q), RANK), :] = passes(split(blocks[q][:, : 4 * RANK]), right)


def lift_kernel(*refs):
    blocks, out = refs[:4], refs[4]
    total = times(blocks[0][:, 4 * RANK :].T, blocks[0][:, : 4 * RANK])
    for q in range(1, 4):
        total = total + times(blocks[q][:, 4 * RANK :].T, blocks[q][:, : 4 * RANK])
    out[...] = total.T


def sum_kernel(tiles, out):
    out[...] = jnp.broadcast_to(jnp.sum(tiles[...], axis=0)[None], (16, 16, RANK))


def top_kernel(gathered, capacitance, out):
    wide = jnp.concatenate([gathered[g] for g in range(16)], axis=1)
    share = times(wide, capacitance[...], 1)
    out[...] = jnp.broadcast_to(share[None], (16, 16, RANK))


def inner_kernel(local, solved, coef, inner):
    inner[...] = local[...] - times(solved[...], coef[...])


def solved_of(inner, top_solved, top_coef):
    return inner[...] - times(top_solved[...], top_coef[...].reshape(CLASSES, RANK), 1)


def next_kernel(
    labels, inner, top_solved, top_coef, inverse, basis, top, lift, local, scaled, coeffs, tiles
):
    sign = signs(labels[...])
    moved = sign * solved_of(inner, top_solved, top_coef)
    box = jnp.clip(moved, 0.0, 1.0)
    rest = moved - box
    scaled[...] = rest
    found = times(inverse[...], sign * (1.0 + (box - rest)))
    local[...] = found
    parts = split(found)
    mine = passes(split(basis[...].T), parts)
    coeffs[...] = mine
    tiles[...] = as_tiles(passes(split(top[...].T), parts) - times(lift[...].T, mine))


def last_kernel(labels, inner, top_solved, top_coef, scaled, box_out, scaled_out):
    moved = scaled[...] + signs(labels[...]) * solved_of(inner, top_solved, top_coef)
    box = jnp.clip(moved, 0.0, 1.0)
    box_out[...] = box
    scaled_out[...] = moved - box


def call(kernel, outs, *args, scratch=(), flops=0):
    shapes = [jax.ShapeDtypeStruct(shape, jnp.float32) for shape in outs]
    moved = sum(4 * a.size for a in args) + sum(4 * s.size for s in shapes)
    return pl.pallas_call(
        kernel,
        out_shape=shapes,
        in_specs=[pl.BlockSpec(memory_space=pltpu.VMEM)] * len(args),
        out_specs=[pl.BlockSpec(memory_space=pltpu.VMEM)] * len(outs),
        scratch_shapes=[pltpu.VMEM(shape, jnp.float32) for shape in scratch],
        compiler_params=pltpu.CompilerParams(vmem_limit_bytes=24 * 1024 * 1024),
        cost_estimate=pl.CostEstimate(flops=flops, bytes_accessed=moved, transcendentals=0),
    )(*args)


STACK = (4 * RANK, CLASSES)
WIDE = (LEAF, CLASSES)
TILES = (16, 16, RANK)
COEFFS = (RANK, CLASSES)
UNIT = 6 * RANK * RANK * RANK


def exchange(tiles, axis):
    return lax.all_to_all(tiles, axis, 0, 0, tiled=True)


def scattered(value, groups):
    return lax.psum_scatter(
        value, BOTH, scatter_dimension=0, axis_index_groups=groups, tiled=True
    )


def along_stride(coeffs):
    return [coeffs] + [lax.ppermute(coeffs, BOTH, stride_pairs(k)) for k in range(1, 4)]


def top_solve(tiles, top_capacitance):
    (shares,) = call(sum_kernel, [TILES], exchange(tiles, "leaf"))
    (coefs,) = call(
        top_kernel, [TILES], exchange(shares, "grp"), top_capacitance, flops=16 * UNIT
    )
    return exchange(coefs, "leaf")


def shards(
    labels,
    leaf_inverse,
    leaf_basis,
    leaf_solved,
    group_capacitance,
    top_basis,
    top_solved,
    top_capacitance,
):
    labels = labels.reshape(1, LEAF)
    pieces = call(
        cut_kernel,
        [(RANK, 5 * RANK)] * 4,
        group_capacitance,
        leaf_solved,
        top_basis,
        flops=4 * UNIT,
    )
    blocks = [pieces[0]] + [lax.ppermute(pieces[q], BOTH, square_pairs(q)) for q in range(1, 4)]

    local, coeffs, projection = call(
        first_kernel,
        [WIDE, COEFFS, COEFFS],
        labels,
        leaf_inverse,
        leaf_basis,
        top_basis,
        flops=48 * UNIT,
    )
    partial, tiles = call(
        group_kernel,
        [STACK, TILES],
        *blocks,
        *along_stride(coeffs),
        projection,
        scratch=[STACK],
        flops=40 * UNIT,
    )
    group_coef = scattered(partial, square_groups())
    (lifts,) = call(lift_kernel, [(4 * RANK, RANK)], *blocks, flops=16 * UNIT)
    lift = scattered(lifts, stride_groups())
    top_coef = top_solve(tiles, top_capacitance)
    (inner,) = call(inner_kernel, [WIDE], local, leaf_solved, group_coef, flops=8 * UNIT)

    local, scaled, coeffs, tiles = call(
        next_kernel,
        [WIDE, WIDE, COEFFS, TILES],
        labels,
        inner,
        top_solved,
        top_coef,
        leaf_inverse,
        leaf_basis,
        top_basis,
        lift,
        flops=60 * UNIT,
    )
    (partial,) = call(
        later_group_kernel,
        [STACK],
        *blocks,
        *along_stride(coeffs),
        scratch=[STACK],
        flops=32 * UNIT,
    )
    group_coef = scattered(partial, square_groups())
    top_coef = top_solve(tiles, top_capacitance)
    (inner,) = call(inner_kernel, [WIDE], local, leaf_solved, group_coef, flops=8 * UNIT)
    return tuple(
        call(
            last_kernel,
            [WIDE, WIDE],
            labels,
            inner,
            top_solved,
            top_coef,
            scaled,
            flops=8 * UNIT,
        )
    )


def solution(mesh):
    rows = P(BOTH, None)
    return jax.shard_map(
        shards,
        mesh=mesh,
        in_specs=(P(BOTH), rows, rows, rows, rows, rows, rows, P("grp", None)),
        out_specs=(rows, rows),
        check_vma=False,
    )
```

```python
import functools

import jax
import jax.numpy as jnp
from jax import lax
from jax.experimental import pallas as pl
from jax.experimental.pallas import tpu as pltpu
from jax.sharding import PartitionSpec as P

CLASSES = 256
RANK = 128
LEAF = 512
BOTH = ("grp", "leaf")


def partner(core, z):
    return (((z + core) ^ 1) - core) % 8


def devices():
    return [(g, i // 8, i % 8) for g in range(16) for i in range(16)]


def index(g, x, z):
    return g * 16 + x * 8 + z


def square_pairs(q):
    pairs = []
    for g, x, z in devices():
        other = index(g, x ^ (q // 2), partner(g % 2, z) if q % 2 else z)
        pairs.append((index(g, x, z), other))
    return pairs


def mirrored_pairs(k):
    sign = (1, -1)
    return [
        (index(g, x, z), index(g, x, (z + 2 * k * sign[g % 2]) % 8)) for g, x, z in devices()
    ]


def split(value):
    high = value.astype(jnp.bfloat16)
    return high, (value - high.astype(jnp.float32)).astype(jnp.bfloat16)


def passes(left, right, right_dim=0):
    def one(a, b):
        return lax.dot_general(
            a, b, (((1,), (right_dim,)), ((), ())), preferred_element_type=jnp.float32
        )

    total = one(left[1], right[0])
    if right[1] is not None:
        total = total + one(left[0], right[1])
    return total + one(left[0], right[0])


def times(left, right, right_dim=0):
    return passes(split(left), split(right), right_dim)


def signs(labels):
    spread = jnp.broadcast_to(labels.astype(jnp.float32), (RANK, LEAF)).T
    lane = lax.broadcasted_iota(jnp.int32, (LEAF, RANK), 1).astype(jnp.float32)
    halves = [jnp.where(spread == lane + RANK * h, 1.0, -1.0) for h in range(2)]
    return jnp.concatenate(halves, axis=1).astype(jnp.float32)


def cut_kernel(capacitance, *refs):
    pieces, done = refs[:4], refs[4]
    leaf = lax.axis_index("leaf")
    x, z = leaf // 8, leaf % 8
    copies = []
    for q in (3, 2, 1, 0):
        first = ((x + q // 2) % 2) * 8 + (z + q) % 2
        for j in range(4):
            start = pl.multiple_of((first + 2 * j) * RANK, RANK)
            copies.append(
                pltpu.make_async_copy(
                    capacitance.at[:, pl.ds(start, RANK)],
                    pieces[q].at[:, j * RANK : (j + 1) * RANK],
                    done.at[4 * q + j],
                )
            )
            copies[-1].start()
    for copy in copies:
        copy.wait()


def first_kernel(labels, inverse, basis, local, coeffs):
    sign = signs(labels[...])
    found = passes(split(inverse[...]), (sign.astype(jnp.bfloat16), None))
    local[...] = found
    coeffs[...] = times(basis[...].T, found)


def row_of(k):
    sign = 1 - 2 * (lax.axis_index("grp") % 2)
    step = (lax.axis_index("leaf") % 8) // 2
    return pl.ds(pl.multiple_of(((step + k * sign + 4) % 4) * RANK, RANK), RANK)


def group_kernel(*refs):
    blocks, pieces, partials, stacked = refs[:4], refs[4:8], refs[8:12], refs[12]
    for piece, k in zip(pieces, (0, -1, 1, 2)):
        stacked[row_of(k), :] = piece[...]
    right = split(stacked[...])
    for q in range(4):
        partials[q][...] = passes(split(blocks[q][...]), right)


def inner_kernel(local, solved, top, *refs):
    parts, inner, tiles = refs[:4], refs[4], refs[5]
    coef = (parts[0][...] + parts[1][...]) + (parts[2][...] + parts[3][...])
    found = local[...] - times(solved[...], coef)
    inner[...] = found
    tiles[...] = times(top[...].T, found).T.reshape(16, 16, RANK)


def sum_kernel(tiles, out):
    out[...] = jnp.broadcast_to(jnp.sum(tiles[...], axis=0)[None], (16, 16, RANK))


def top_kernel(gathered, capacitance, out):
    wide = jnp.concatenate([gathered[g] for g in range(16)], axis=1)
    share = times(wide, capacitance[...], 1)
    out[...] = jnp.broadcast_to(share[None], (16, 16, RANK))


def solved_of(inner, top_solved, top_coef):
    return inner[...] - times(top_solved[...], top_coef[...].reshape(CLASSES, RANK), 1)


def next_kernel(
    inner, top_coef, labels, top_solved, inverse, basis, local, scaled, coeffs
):
    sign = signs(labels[...])
    moved = sign * solved_of(inner, top_solved, top_coef)
    box = jnp.clip(moved, 0.0, 1.0)
    rest = moved - box
    scaled[...] = rest
    found = times(inverse[...], sign * (1.0 + (box - rest)))
    local[...] = found
    coeffs[...] = times(basis[...].T, found)


def last_kernel(inner, top_coef, scaled, labels, top_solved, box_out, scaled_out):
    moved = scaled[...] + signs(labels[...]) * solved_of(inner, top_solved, top_coef)
    box = jnp.clip(moved, 0.0, 1.0)
    box_out[...] = box
    scaled_out[...] = moved - box


def call(kernel, outs, args, scratch=(), flops=0):
    shapes = [jax.ShapeDtypeStruct(shape, jnp.float32) for shape in outs]
    moved = sum(4 * a.size for a in args) + sum(4 * s.size for s in shapes)
    return pl.pallas_call(
        kernel,
        out_shape=shapes,
        in_specs=[pl.BlockSpec(memory_space=pltpu.VMEM)] * len(args),
        out_specs=[pl.BlockSpec(memory_space=pltpu.VMEM)] * len(outs),
        scratch_shapes=[pltpu.VMEM(shape, jnp.float32) for shape in scratch],
        compiler_params=pltpu.CompilerParams(vmem_limit_bytes=16 * 1024 * 1024),
        cost_estimate=pl.CostEstimate(flops=flops, bytes_accessed=moved, transcendentals=0),
    )(*args)


STACK = (4 * RANK, CLASSES)
WIDE = (LEAF, CLASSES)
TILES = (16, 16, RANK)
COEFFS = (RANK, CLASSES)
UNIT = 6 * RANK * RANK * RANK


def exchange(tiles, axis):
    return lax.all_to_all(tiles, axis, 0, 0, tiled=True)


def across_square(pieces):
    return [pieces[0]] + [lax.ppermute(pieces[q], BOTH, square_pairs(q)) for q in range(1, 4)]


def relayed(coeffs):
    before = lax.ppermute(coeffs, BOTH, mirrored_pairs(1))
    after = lax.ppermute(coeffs, BOTH, mirrored_pairs(-1))
    opposite = lax.ppermute(before, BOTH, mirrored_pairs(1))
    return [coeffs, before, after, opposite]


def iteration(local, coeffs, blocks, leaf_solved, top_basis, top_capacitance):
    partials = call(
        group_kernel,
        [COEFFS] * 4,
        [*blocks, *relayed(coeffs)],
        scratch=[STACK],
        flops=32 * UNIT,
    )
    inner, tiles = call(
        inner_kernel,
        [WIDE, TILES],
        [local, leaf_solved, top_basis, *across_square(partials)],
        flops=16 * UNIT,
    )
    (shares,) = call(sum_kernel, [TILES], [exchange(tiles, "leaf")])
    (coefs,) = call(
        top_kernel, [TILES], [exchange(shares, "grp"), top_capacitance], flops=16 * UNIT
    )
    return inner, exchange(coefs, "leaf")


def shards(
    labels,
    leaf_inverse,
    leaf_basis,
    leaf_solved,
    group_capacitance,
    top_basis,
    top_solved,
    top_capacitance,
):
    labels = labels.reshape(1, LEAF)
    pieces = pl.pallas_call(
        cut_kernel,
        out_shape=[jax.ShapeDtypeStruct((RANK, 4 * RANK), jnp.float32)] * 4,
        in_specs=[pl.BlockSpec(memory_space=pl.ANY)],
        out_specs=[pl.BlockSpec(memory_space=pl.ANY)] * 4,
        scratch_shapes=[pltpu.SemaphoreType.DMA((16,))],
        compiler_params=pltpu.CompilerParams(vmem_limit_bytes=16 * 1024 * 1024),
    )(group_capacitance)
    blocks = across_square(pieces)
    local, coeffs = call(
        first_kernel,
        [WIDE, COEFFS],
        [labels, leaf_inverse, leaf_basis],
        flops=40 * UNIT,
    )
    shared = (blocks, leaf_solved, top_basis, top_capacitance)
    inner, top_coef = iteration(local, coeffs, *shared)
    local, scaled, coeffs = call(
        next_kernel,
        [WIDE, WIDE, COEFFS],
        [inner, top_coef, labels, top_solved, leaf_inverse, leaf_basis],
        flops=56 * UNIT,
    )
    inner, top_coef = iteration(local, coeffs, *shared)
    return tuple(
        call(
            last_kernel, [WIDE, WIDE], [inner, top_coef, scaled, labels, top_solved], flops=8 * UNIT
        )
    )


def solution(mesh):
    rows = P(BOTH, None)
    return jax.shard_map(
        shards,
        mesh=mesh,
        in_specs=(P(BOTH), rows, rows, rows, rows, rows, rows, P("grp", None)),
        out_specs=(rows, rows),
        check_vma=False,
    )
```

```python
import functools

import jax
import jax.numpy as jnp
from jax import lax
from jax.experimental import pallas as pl
from jax.experimental.pallas import tpu as pltpu
from jax.sharding import PartitionSpec as P

CLASSES = 256
RANK = 128
LEAF = 512
BOTH = ("grp", "leaf")


def partner(core, z):
    return (((z + core) ^ 1) - core) % 8


def devices():
    return [(g, i // 8, i % 8) for g in range(16) for i in range(16)]


def index(g, x, z):
    return g * 16 + x * 8 + z


def square_pairs(q):
    pairs = []
    for g, x, z in devices():
        other = index(g, x ^ (q // 2), partner(g % 2, z) if q % 2 else z)
        pairs.append((index(g, x, z), other))
    return pairs


def mirrored_pairs(k):
    sign = (1, -1)
    return [
        (index(g, x, z), index(g, x, (z + 2 * k * sign[g % 2]) % 8)) for g, x, z in devices()
    ]


def split(value):
    high = value.astype(jnp.bfloat16)
    return high, (value - high.astype(jnp.float32)).astype(jnp.bfloat16)


def passes(left, right, right_dim=0):
    def one(a, b):
        return lax.dot_general(
            a, b, (((1,), (right_dim,)), ((), ())), preferred_element_type=jnp.float32
        )

    total = one(left[1], right[0])
    if right[1] is not None:
        total = total + one(left[0], right[1])
    return total + one(left[0], right[0])


def times(left, right, right_dim=0):
    return passes(split(left), split(right), right_dim)


def signs(labels):
    spread = jnp.broadcast_to(labels.astype(jnp.float32), (RANK, LEAF)).T
    lane = lax.broadcasted_iota(jnp.int32, (LEAF, RANK), 1).astype(jnp.float32)
    halves = [jnp.where(spread == lane + RANK * h, 1.0, -1.0) for h in range(2)]
    return jnp.concatenate(halves, axis=1).astype(jnp.float32)


def cut_kernel(capacitance, *refs):
    pieces, done = refs[:4], refs[4]
    leaf = lax.axis_index("leaf")
    x, z = leaf // 8, leaf % 8
    copies = []
    for q in (3, 2, 1, 0):
        first = ((x + q // 2) % 2) * 8 + (z + q) % 2
        for j in range(4):
            start = pl.multiple_of((first + 2 * j) * RANK, RANK)
            copies.append(
                pltpu.make_async_copy(
                    capacitance.at[:, pl.ds(start, RANK)],
                    pieces[q].at[:, j * RANK : (j + 1) * RANK],
                    done.at[4 * q + j],
                )
            )
            copies[-1].start()
    for copy in copies:
        copy.wait()


def first_kernel(labels, inverse, basis, local, coeffs):
    sign = signs(labels[...])
    found = passes(split(inverse[...]), (sign.astype(jnp.bfloat16), None))
    local[...] = found
    coeffs[...] = times(basis[...].T, found)


def lift_kernel(solved, top, lift):
    found = times(top[...].T, solved[...])
    lift[...] = jnp.concatenate([found[: RANK // 2], found[RANK // 2 :]], axis=1)


def row_of(k):
    sign = 1 - 2 * (lax.axis_index("grp") % 2)
    step = (lax.axis_index("leaf") % 8) // 2
    return pl.ds(pl.multiple_of(((step + k * sign + 4) % 4) * RANK, RANK), RANK)


def partial_coefs(blocks, pieces, stacked):
    for piece, k in zip(pieces, (0, -1, 1, 2)):
        stacked[row_of(k), :] = piece[...]
    block = jnp.concatenate([part[...] for part in blocks], axis=0)
    return passes(split(block), split(stacked[...]))


def group_kernel(lift, *refs):
    rows = partial_coefs(refs[:4], refs[4:8], refs[12])
    for q in range(4):
        refs[8 + q][:RANK, :] = rows[q * RANK : (q + 1) * RANK]
        refs[8 + q][RANK:, :] = lift[...]


def inner_kernel(local, solved, top, *refs):
    parts, inner, tiles = refs[:4], refs[4], refs[5]
    coef = (parts[0][:RANK] + parts[1][:RANK]) + (parts[2][:RANK] + parts[3][:RANK])
    found = local[...] - times(solved[...], coef)
    inner[...] = found
    tiles[...] = times(top[...].T, found).T.reshape(16, 16, RANK)


def later_group_kernel(projection, *refs):
    sent, partials, tiles = refs[8:12], refs[12:16], refs[16]
    rows = partial_coefs(refs[:4], refs[4:8], refs[17])
    lifts = []
    for q in range(4):
        partials[q][...] = rows[q * RANK : (q + 1) * RANK]
        lift = sent[q][RANK:, :]
        lifts.append(jnp.concatenate([lift[:, :RANK], lift[:, RANK:]], axis=0))
    total = projection[...] - times(jnp.concatenate(lifts, axis=1), rows)
    tiles[...] = total.T.reshape(16, 16, RANK)


def sum_inner_kernel(tiles, local, solved, *refs):
    parts, out, inner = refs[:4], refs[4], refs[5]
    out[...] = jnp.broadcast_to(jnp.sum(tiles[...], axis=0)[None], (16, 16, RANK))
    coef = (parts[0][...] + parts[1][...]) + (parts[2][...] + parts[3][...])
    inner[...] = local[...] - times(solved[...], coef)


def sum_kernel(tiles, out):
    out[...] = jnp.broadcast_to(jnp.sum(tiles[...], axis=0)[None], (16, 16, RANK))


def top_kernel(gathered, capacitance, out):
    wide = jnp.concatenate([gathered[g] for g in range(16)], axis=1)
    share = times(wide, capacitance[...], 1)
    out[...] = jnp.broadcast_to(share[None], (16, 16, RANK))


def solved_of(inner, top_solved, top_coef):
    return inner[...] - times(top_solved[...], top_coef[...].reshape(CLASSES, RANK), 1)


def next_kernel(
    inner, top_coef, labels, top_solved, inverse, basis, top, local, scaled, coeffs, projection
):
    sign = signs(labels[...])
    moved = sign * solved_of(inner, top_solved, top_coef)
    box = jnp.clip(moved, 0.0, 1.0)
    rest = moved - box
    scaled[...] = rest
    found = times(inverse[...], sign * (1.0 + (box - rest)))
    local[...] = found
    parts = split(found)
    coeffs[...] = passes(split(basis[...].T), parts)
    projection[...] = passes(split(top[...].T), parts)


def last_kernel(inner, top_coef, scaled, labels, top_solved, box_out, scaled_out):
    moved = scaled[...] + signs(labels[...]) * solved_of(inner, top_solved, top_coef)
    box = jnp.clip(moved, 0.0, 1.0)
    box_out[...] = box
    scaled_out[...] = moved - box


def call(kernel, outs, args, scratch=(), flops=0):
    shapes = [jax.ShapeDtypeStruct(shape, jnp.float32) for shape in outs]
    moved = sum(4 * a.size for a in args) + sum(4 * s.size for s in shapes)
    return pl.pallas_call(
        kernel,
        out_shape=shapes,
        in_specs=[pl.BlockSpec(memory_space=pltpu.VMEM)] * len(args),
        out_specs=[pl.BlockSpec(memory_space=pltpu.VMEM)] * len(outs),
        scratch_shapes=[pltpu.VMEM(shape, jnp.float32) for shape in scratch],
        compiler_params=pltpu.CompilerParams(vmem_limit_bytes=16 * 1024 * 1024),
        cost_estimate=pl.CostEstimate(flops=flops, bytes_accessed=moved, transcendentals=0),
    )(*args)


STACK = (4 * RANK, CLASSES)
WIDE = (LEAF, CLASSES)
TILES = (16, 16, RANK)
COEFFS = (RANK, CLASSES)
UNIT = 6 * RANK * RANK * RANK


def exchange(tiles, axis):
    return lax.all_to_all(tiles, axis, 0, 0, tiled=True)


def across_square(pieces):
    return [pieces[0]] + [lax.ppermute(pieces[q], BOTH, square_pairs(q)) for q in range(1, 4)]


def relayed(coeffs):
    before = lax.ppermute(coeffs, BOTH, mirrored_pairs(1))
    after = lax.ppermute(coeffs, BOTH, mirrored_pairs(-1))
    opposite = lax.ppermute(before, BOTH, mirrored_pairs(1))
    return [coeffs, before, after, opposite]


def top_solve(shares, top_capacitance):
    (coefs,) = call(
        top_kernel, [TILES], [exchange(shares, "grp"), top_capacitance], flops=16 * UNIT
    )
    return exchange(coefs, "leaf")


def shards(
    labels,
    leaf_inverse,
    leaf_basis,
    leaf_solved,
    group_capacitance,
    top_basis,
    top_solved,
    top_capacitance,
):
    labels = labels.reshape(1, LEAF)
    pieces = pl.pallas_call(
        cut_kernel,
        out_shape=[jax.ShapeDtypeStruct((RANK, 4 * RANK), jnp.float32)] * 4,
        in_specs=[pl.BlockSpec(memory_space=pl.ANY)],
        out_specs=[pl.BlockSpec(memory_space=pl.ANY)] * 4,
        scratch_shapes=[pltpu.SemaphoreType.DMA((16,))],
        compiler_params=pltpu.CompilerParams(vmem_limit_bytes=16 * 1024 * 1024),
    )(group_capacitance)
    blocks = across_square(pieces)
    local, coeffs = call(
        first_kernel,
        [WIDE, COEFFS],
        [labels, leaf_inverse, leaf_basis],
        flops=40 * UNIT,
    )
    (lift,) = call(lift_kernel, [(RANK // 2, CLASSES)], [leaf_solved, top_basis], flops=4 * UNIT)
    sent = across_square(
        call(
            group_kernel,
            [(RANK + RANK // 2, CLASSES)] * 4,
            [lift, *blocks, *relayed(coeffs)],
            scratch=[STACK],
            flops=32 * UNIT,
        )
    )
    inner, tiles = call(
        inner_kernel,
        [WIDE, TILES],
        [local, leaf_solved, top_basis, *sent],
        flops=16 * UNIT,
    )
    (shares,) = call(sum_kernel, [TILES], [exchange(tiles, "leaf")])
    top_coef = top_solve(shares, top_capacitance)

    local, scaled, coeffs, projection = call(
        next_kernel,
        [WIDE, WIDE, COEFFS, COEFFS],
        [inner, top_coef, labels, top_solved, leaf_inverse, leaf_basis, top_basis],
        flops=56 * UNIT,
    )
    *partials, tiles = call(
        later_group_kernel,
        [COEFFS] * 4 + [TILES],
        [projection, *blocks, *relayed(coeffs), *sent],
        scratch=[STACK],
        flops=40 * UNIT,
    )
    shares, inner = call(
        sum_inner_kernel,
        [TILES, WIDE],
        [exchange(tiles, "leaf"), local, leaf_solved, *across_square(partials)],
        flops=8 * UNIT,
    )
    top_coef = top_solve(shares, top_capacitance)
    return tuple(
        call(
            last_kernel, [WIDE, WIDE], [inner, top_coef, scaled, labels, top_solved], flops=8 * UNIT
        )
    )


def solution(mesh):
    rows = P(BOTH, None)
    return jax.shard_map(
        shards,
        mesh=mesh,
        in_specs=(P(BOTH), rows, rows, rows, rows, rows, rows, P("grp", None)),
        out_specs=(rows, rows),
        check_vma=False,
    )
```

```python
import functools

import jax
import jax.numpy as jnp
from jax import lax
from jax.experimental import pallas as pl
from jax.experimental.pallas import tpu as pltpu
from jax.sharding import PartitionSpec as P

CLASSES = 256
RANK = 128
LEAF = 512
BOTH = ("grp", "leaf")


def partner(core, z):
    return (((z + core) ^ 1) - core) % 8


def devices():
    return [(g, i // 8, i % 8) for g in range(16) for i in range(16)]


def index(g, x, z):
    return g * 16 + x * 8 + z


def square_pairs(q):
    pairs = []
    for g, x, z in devices():
        other = index(g, x ^ (q // 2), partner(g % 2, z) if q % 2 else z)
        pairs.append((index(g, x, z), other))
    return pairs


def mirrored_pairs(k):
    sign = (1, -1)
    return [
        (index(g, x, z), index(g, x, (z + 2 * k * sign[g % 2]) % 8)) for g, x, z in devices()
    ]


def split(value):
    high = value.astype(jnp.bfloat16)
    return high, (value - high.astype(jnp.float32)).astype(jnp.bfloat16)


def passes(left, right, right_dim=0):
    def one(a, b):
        return lax.dot_general(
            a, b, (((1,), (right_dim,)), ((), ())), preferred_element_type=jnp.float32
        )

    total = one(left[1], right[0])
    if right[1] is not None:
        total = total + one(left[0], right[1])
    return total + one(left[0], right[0])


def times(left, right, right_dim=0):
    return passes(split(left), split(right), right_dim)


def signs(labels):
    spread = jnp.broadcast_to(labels.astype(jnp.float32), (RANK, LEAF)).T
    lane = lax.broadcasted_iota(jnp.int32, (LEAF, RANK), 1).astype(jnp.float32)
    halves = [jnp.where(spread == lane + RANK * h, 1.0, -1.0) for h in range(2)]
    return jnp.concatenate(halves, axis=1).astype(jnp.float32)


def cut_kernel(capacitance, *refs):
    pieces, done = refs[:4], refs[4]
    leaf = lax.axis_index("leaf")
    x, z = leaf // 8, leaf % 8
    copies = []
    for q in (3, 2, 1, 0):
        first = ((x + q // 2) % 2) * 8 + (z + q) % 2
        for j in range(4):
            start = pl.multiple_of((first + 2 * j) * RANK, RANK)
            copies.append(
                pltpu.make_async_copy(
                    capacitance.at[:, pl.ds(start, RANK)],
                    pieces[q].at[:, j * RANK : (j + 1) * RANK],
                    done.at[4 * q + j],
                )
            )
            copies[-1].start()
    for copy in copies:
        copy.wait()


def first_kernel(labels, inverse, basis, local, coeffs):
    sign = signs(labels[...])
    found = passes(split(inverse[...]), (sign.astype(jnp.bfloat16), None))
    local[...] = found
    coeffs[...] = times(basis[...].T, found)


def lift_kernel(solved, top, lift, folded):
    found = times(top[...].T, solved[...])
    lift[...] = found
    folded[...] = jnp.concatenate([found[: RANK // 2], found[RANK // 2 :]], axis=1)


def project_kernel(local, top, projection):
    projection[...] = times(top[...].T, local[...])


def reach_kernel(inverse, basis, top, reach):
    both = jnp.concatenate([basis[...].T, top[...].T], axis=0)
    reach[...] = times(both, inverse[...])


def block_lift_kernel(*refs):
    blocks, sent, out = refs[:4], refs[4:8], refs[8]
    lifts = []
    for q in range(4):
        lift = sent[q][RANK:, :]
        lifts.append(jnp.concatenate([lift[:, :RANK], lift[:, RANK:]], axis=0))
    block = jnp.concatenate([part[...] for part in blocks], axis=0)
    out[...] = times(jnp.concatenate(lifts, axis=1), block)


def row_of(k):
    sign = 1 - 2 * (lax.axis_index("grp") % 2)
    step = (lax.axis_index("leaf") % 8) // 2
    return pl.ds(pl.multiple_of(((step + k * sign + 4) % 4) * RANK, RANK), RANK)


def partial_coefs(blocks, pieces, stacked):
    for piece, k in zip(pieces, (0, -1, 1, 2)):
        stacked[row_of(k), :] = piece[...]
    block = jnp.concatenate([part[...] for part in blocks], axis=0)
    return passes(split(block), split(stacked[...]))


def group_kernel(lift, *refs):
    rows = partial_coefs(refs[:4], refs[4:8], refs[12])
    for q in range(4):
        refs[8 + q][:RANK, :] = rows[q * RANK : (q + 1) * RANK]
        refs[8 + q][RANK:, :] = lift[...]


def inner_kernel(local, solved, lift, projection, reach, *refs):
    parts, inner, tiles = refs[:4], refs[4], refs[5]
    coef = (parts[0][:RANK] + parts[1][:RANK]) + (parts[2][:RANK] + parts[3][:RANK])
    both = times(jnp.concatenate([solved[...], lift[...]], axis=0), coef)
    inner[...] = local[...] - both[:LEAF]
    tiles[...] = (projection[...] - both[LEAF:]).T.reshape(16, 16, RANK)


def later_group_kernel(projection, block_lift, *refs):
    partials, tiles = refs[8:12], refs[12]
    rows = partial_coefs([*refs[:4], block_lift], refs[4:8], refs[13])
    for q in range(4):
        partials[q][...] = rows[q * RANK : (q + 1) * RANK]
    tiles[...] = (projection[...] - rows[4 * RANK :]).T.reshape(16, 16, RANK)


def sum_inner_kernel(tiles, local, solved, *refs):
    parts, out, inner = refs[:4], refs[4], refs[5]
    out[...] = jnp.broadcast_to(jnp.sum(tiles[...], axis=0)[None], (16, 16, RANK))
    coef = (parts[0][...] + parts[1][...]) + (parts[2][...] + parts[3][...])
    inner[...] = local[...] - times(solved[...], coef)


def sum_kernel(tiles, out):
    out[...] = jnp.broadcast_to(jnp.sum(tiles[...], axis=0)[None], (16, 16, RANK))


def top_kernel(gathered, capacitance, out):
    wide = jnp.concatenate([gathered[g] for g in range(16)], axis=1)
    share = times(wide, capacitance[...], 1)
    out[...] = jnp.broadcast_to(share[None], (16, 16, RANK))


def solved_of(inner, top_solved, top_coef):
    return inner[...] - times(top_solved[...], top_coef[...].reshape(CLASSES, RANK), 1)


def next_kernel(
    inner, top_coef, labels, top_solved, inverse, reach, local, scaled, coeffs, projection
):
    sign = signs(labels[...])
    moved = sign * solved_of(inner, top_solved, top_coef)
    box = jnp.clip(moved, 0.0, 1.0)
    rest = moved - box
    scaled[...] = rest
    both = jnp.concatenate([inverse[...], reach[...]], axis=0)
    found = times(both, sign * (1.0 + (box - rest)))
    local[...] = found[:LEAF]
    coeffs[...] = found[LEAF : LEAF + RANK]
    projection[...] = found[LEAF + RANK :]


def last_kernel(inner, top_coef, scaled, labels, top_solved, box_out, scaled_out, near, done):
    right = split(top_coef[...].reshape(CLASSES, RANK))
    sign = signs(labels[...])
    half = LEAF // 2
    copies = []
    for part in range(2):
        rows = slice(part * half, (part + 1) * half)
        solved = inner[rows] - passes(split(top_solved[rows]), right, 1)
        moved = scaled[rows] + sign[rows] * solved
        box = jnp.clip(moved, 0.0, 1.0)
        near[0, rows] = box
        near[1, rows] = moved - box
        for i, out in enumerate((box_out, scaled_out)):
            copy = pltpu.make_async_copy(near.at[i, rows], out.at[rows], done.at[2 * part + i])
            copy.start()
            copies.append(copy)
    for copy in copies:
        copy.wait()


def call(kernel, outs, args, scratch=(), flops=0):
    shapes = [jax.ShapeDtypeStruct(shape, jnp.float32) for shape in outs]
    moved = sum(4 * a.size for a in args) + sum(4 * s.size for s in shapes)
    return pl.pallas_call(
        kernel,
        out_shape=shapes,
        in_specs=[pl.BlockSpec(memory_space=pltpu.VMEM)] * len(args),
        out_specs=[pl.BlockSpec(memory_space=pltpu.VMEM)] * len(outs),
        scratch_shapes=[pltpu.VMEM(shape, jnp.float32) for shape in scratch],
        compiler_params=pltpu.CompilerParams(vmem_limit_bytes=16 * 1024 * 1024),
        cost_estimate=pl.CostEstimate(flops=flops, bytes_accessed=moved, transcendentals=0),
    )(*args)


STACK = (4 * RANK, CLASSES)
WIDE = (LEAF, CLASSES)
TILES = (16, 16, RANK)
COEFFS = (RANK, CLASSES)
UNIT = 6 * RANK * RANK * RANK


def exchange(tiles, axis):
    return lax.all_to_all(tiles, axis, 0, 0, tiled=True)


def across_square(pieces):
    return [pieces[0]] + [lax.ppermute(pieces[q], BOTH, square_pairs(q)) for q in range(1, 4)]


def relayed(coeffs):
    before = lax.ppermute(coeffs, BOTH, mirrored_pairs(1))
    after = lax.ppermute(coeffs, BOTH, mirrored_pairs(-1))
    opposite = lax.ppermute(before, BOTH, mirrored_pairs(1))
    return [coeffs, before, after, opposite]


def top_solve(shares, top_capacitance):
    (coefs,) = call(
        top_kernel, [TILES], [exchange(shares, "grp"), top_capacitance], flops=16 * UNIT
    )
    return exchange(coefs, "leaf")


def shards(
    labels,
    leaf_inverse,
    leaf_basis,
    leaf_solved,
    group_capacitance,
    top_basis,
    top_solved,
    top_capacitance,
):
    labels = labels.reshape(1, LEAF)
    pieces = pl.pallas_call(
        cut_kernel,
        out_shape=[jax.ShapeDtypeStruct((RANK, 4 * RANK), jnp.float32)] * 4,
        in_specs=[pl.BlockSpec(memory_space=pl.ANY)],
        out_specs=[pl.BlockSpec(memory_space=pl.ANY)] * 4,
        scratch_shapes=[pltpu.SemaphoreType.DMA((16,))],
        compiler_params=pltpu.CompilerParams(vmem_limit_bytes=16 * 1024 * 1024),
    )(group_capacitance)
    blocks = across_square(pieces)
    local, coeffs = call(
        first_kernel,
        [WIDE, COEFFS],
        [labels, leaf_inverse, leaf_basis],
        flops=40 * UNIT,
    )
    lift, folded = call(
        lift_kernel,
        [(RANK, RANK), (RANK // 2, CLASSES)],
        [leaf_solved, top_basis],
        flops=4 * UNIT,
    )
    (projection,) = call(project_kernel, [COEFFS], [local, top_basis], flops=8 * UNIT)
    (reach,) = call(
        reach_kernel,
        [(2 * RANK, LEAF)],
        [leaf_inverse, leaf_basis, top_basis],
        flops=32 * UNIT,
    )
    sent = across_square(
        call(
            group_kernel,
            [(RANK + RANK // 2, CLASSES)] * 4,
            [folded, *blocks, *relayed(coeffs)],
            scratch=[STACK],
            flops=32 * UNIT,
        )
    )
    inner, tiles = call(
        inner_kernel,
        [WIDE, TILES],
        [local, leaf_solved, lift, projection, reach, *sent],
        flops=10 * UNIT,
    )
    (shares,) = call(sum_kernel, [TILES], [exchange(tiles, "leaf")])
    top_coef = top_solve(shares, top_capacitance)

    local, scaled, coeffs, projection = call(
        next_kernel,
        [WIDE, WIDE, COEFFS, COEFFS],
        [inner, top_coef, labels, top_solved, leaf_inverse, reach],
        flops=56 * UNIT,
    )
    (block_lift,) = call(
        block_lift_kernel, [(RANK, 4 * RANK)], [*blocks, *sent], flops=16 * UNIT
    )
    *partials, tiles = call(
        later_group_kernel,
        [COEFFS] * 4 + [TILES],
        [projection, block_lift, *blocks, *relayed(coeffs)],
        scratch=[STACK],
        flops=40 * UNIT,
    )
    shares, inner = call(
        sum_inner_kernel,
        [TILES, WIDE],
        [exchange(tiles, "leaf"), local, leaf_solved, *across_square(partials)],
        flops=8 * UNIT,
    )
    top_coef = top_solve(shares, top_capacitance)
    return tuple(
        pl.pallas_call(
            last_kernel,
            out_shape=[jax.ShapeDtypeStruct(WIDE, jnp.float32)] * 2,
            in_specs=[pl.BlockSpec(memory_space=pltpu.VMEM)] * 5,
            out_specs=[pl.BlockSpec(memory_space=pl.ANY)] * 2,
            scratch_shapes=[
                pltpu.VMEM((2, *WIDE), jnp.float32),
                pltpu.SemaphoreType.DMA((4,)),
            ],
            compiler_params=pltpu.CompilerParams(vmem_limit_bytes=16 * 1024 * 1024),
        )(inner, top_coef, scaled, labels, top_solved)
    )


def solution(mesh):
    rows = P(BOTH, None)
    return jax.shard_map(
        shards,
        mesh=mesh,
        in_specs=(P(BOTH), rows, rows, rows, rows, rows, rows, P("grp", None)),
        out_specs=(rows, rows),
        check_vma=False,
    )
```

```python
import functools

import jax
import jax.numpy as jnp
from jax import lax
from jax.experimental import pallas as pl
from jax.experimental.pallas import tpu as pltpu
from jax.sharding import PartitionSpec as P

CLASSES = 256
RANK = 128
LEAF = 512
BOTH = ("grp", "leaf")


def partner(core, z):
    return (((z + core) ^ 1) - core) % 8


def devices():
    return [(g, i // 8, i % 8) for g in range(16) for i in range(16)]


def index(g, x, z):
    return g * 16 + x * 8 + z


def square_pairs(q):
    pairs = []
    for g, x, z in devices():
        other = index(g, x ^ (q // 2), partner(g % 2, z) if q % 2 else z)
        pairs.append((index(g, x, z), other))
    return pairs


def mirrored_pairs(k):
    sign = (1, -1)
    return [
        (index(g, x, z), index(g, x, (z + 2 * k * sign[g % 2]) % 8)) for g, x, z in devices()
    ]


def split(value):
    high = value.astype(jnp.bfloat16)
    return high, (value - high.astype(jnp.float32)).astype(jnp.bfloat16)


def passes(left, right, right_dim=0):
    def one(a, b):
        return lax.dot_general(
            a, b, (((1,), (right_dim,)), ((), ())), preferred_element_type=jnp.float32
        )

    total = one(left[1], right[0])
    if right[1] is not None:
        total = total + one(left[0], right[1])
    return total + one(left[0], right[0])


def times(left, right, right_dim=0):
    return passes(split(left), split(right), right_dim)


def signs(labels):
    spread = jnp.broadcast_to(labels.astype(jnp.float32), (RANK, LEAF)).T
    lane = lax.broadcasted_iota(jnp.int32, (LEAF, RANK), 1).astype(jnp.float32)
    halves = [jnp.where(spread == lane + RANK * h, 1.0, -1.0) for h in range(2)]
    return jnp.concatenate(halves, axis=1).astype(jnp.float32)


def cut_kernel(capacitance, *refs):
    pieces, done = refs[:4], refs[4]
    leaf = lax.axis_index("leaf")
    x, z = leaf // 8, leaf % 8
    copies = []
    for q in (3, 2, 1, 0):
        first = ((x + q // 2) % 2) * 8 + (z + q) % 2
        for j in range(4):
            start = pl.multiple_of((first + 2 * j) * RANK, RANK)
            copies.append(
                pltpu.make_async_copy(
                    capacitance.at[:, pl.ds(start, RANK)],
                    pieces[q].at[:, j * RANK : (j + 1) * RANK],
                    done.at[4 * q + j],
                )
            )
            copies[-1].start()
    for copy in copies:
        copy.wait()


def first_kernel(labels, inverse, basis, *refs):
    local_out, coeffs_out, near_labels, near, near_basis, local, coeffs, done = refs
    quarter = LEAF // 4
    parts = [slice(k * quarter, (k + 1) * quarter) for k in range(4)]
    copies = [pltpu.make_async_copy(labels, near_labels, done.at[0])]
    for k, rows in enumerate(parts):
        copies.append(pltpu.make_async_copy(inverse.at[rows], near.at[rows], done.at[k + 1]))
    copies.append(pltpu.make_async_copy(basis, near_basis, done.at[5]))
    for copy in copies:
        copy.start()
    copies[0].wait()
    sign = (signs(near_labels[...]).astype(jnp.bfloat16), None)
    for k, rows in enumerate(parts):
        copies[k + 1].wait()
        local[rows] = passes(split(near[rows]), sign)
    leaving = pltpu.make_async_copy(local, local_out, done.at[6])
    leaving.start()
    copies[5].wait()
    coeffs[...] = times(near_basis[...].T, local[...])
    last = pltpu.make_async_copy(coeffs, coeffs_out, done.at[7])
    last.start()
    leaving.wait()
    last.wait()


def lift_kernel(solved, top, lift, folded):
    found = times(top[...].T, solved[...])
    lift[...] = found
    folded[...] = jnp.concatenate([found[: RANK // 2], found[RANK // 2 :]], axis=1)


def project_kernel(local, top, projection):
    projection[...] = times(top[...].T, local[...])


def reach_kernel(inverse, basis, top, reach):
    both = jnp.concatenate([basis[...].T, top[...].T], axis=0)
    reach[...] = times(both, inverse[...])


def block_lift_kernel(*refs):
    blocks, sent, out = refs[:4], refs[4:8], refs[8]
    lifts = []
    for q in range(4):
        lift = sent[q][RANK:, :]
        lifts.append(jnp.concatenate([lift[:, :RANK], lift[:, RANK:]], axis=0))
    block = jnp.concatenate([part[...] for part in blocks], axis=0)
    out[...] = times(jnp.concatenate(lifts, axis=1), block)


def row_of(k):
    sign = 1 - 2 * (lax.axis_index("grp") % 2)
    step = (lax.axis_index("leaf") % 8) // 2
    return pl.ds(pl.multiple_of(((step + k * sign + 4) % 4) * RANK, RANK), RANK)


def partial_coefs(blocks, pieces, stacked):
    for piece, k in zip(pieces, (0, -1, 1, 2)):
        stacked[row_of(k), :] = piece[...]
    block = jnp.concatenate([part[...] for part in blocks], axis=0)
    return passes(split(block), split(stacked[...]))


def group_kernel(lift, *refs):
    rows = partial_coefs(refs[:4], refs[4:8], refs[12])
    for q in range(4):
        refs[8 + q][:RANK, :] = rows[q * RANK : (q + 1) * RANK]
        refs[8 + q][RANK:, :] = lift[...]


def inner_kernel(local, solved, lift, projection, reach, *refs):
    parts, inner, tiles = refs[:4], refs[4], refs[5]
    coef = (parts[0][:RANK] + parts[1][:RANK]) + (parts[2][:RANK] + parts[3][:RANK])
    both = times(jnp.concatenate([solved[...], lift[...]], axis=0), coef)
    inner[...] = local[...] - both[:LEAF]
    tiles[...] = (projection[...] - both[LEAF:]).T.reshape(16, 16, RANK)


def later_group_kernel(projection, block_lift, *refs):
    partials, tiles = refs[8:12], refs[12]
    rows = partial_coefs([*refs[:4], block_lift], refs[4:8], refs[13])
    for q in range(4):
        partials[q][...] = rows[q * RANK : (q + 1) * RANK]
    tiles[...] = (projection[...] - rows[4 * RANK :]).T.reshape(16, 16, RANK)


def sum_inner_kernel(tiles, local, solved, *refs):
    parts, out, inner = refs[:4], refs[4], refs[5]
    out[...] = jnp.broadcast_to(jnp.sum(tiles[...], axis=0)[None], (16, 16, RANK))
    coef = (parts[0][...] + parts[1][...]) + (parts[2][...] + parts[3][...])
    inner[...] = local[...] - times(solved[...], coef)


def sum_kernel(tiles, out):
    out[...] = jnp.broadcast_to(jnp.sum(tiles[...], axis=0)[None], (16, 16, RANK))


def top_kernel(gathered, capacitance, out):
    wide = jnp.concatenate([gathered[g] for g in range(16)], axis=1)
    share = times(wide, capacitance[...], 1)
    out[...] = jnp.broadcast_to(share[None], (16, 16, RANK))


def solved_of(inner, top_solved, top_coef):
    return inner[...] - times(top_solved[...], top_coef[...].reshape(CLASSES, RANK), 1)


def next_kernel(
    inner, top_coef, labels, top_solved, inverse, reach, local, scaled, coeffs, projection
):
    sign = signs(labels[...])
    moved = sign * solved_of(inner, top_solved, top_coef)
    box = jnp.clip(moved, 0.0, 1.0)
    rest = moved - box
    scaled[...] = rest
    both = jnp.concatenate([inverse[...], reach[...]], axis=0)
    found = times(both, sign * (1.0 + (box - rest)))
    local[...] = found[:LEAF]
    coeffs[...] = found[LEAF : LEAF + RANK]
    projection[...] = found[LEAF + RANK :]


def last_kernel(inner, top_coef, scaled, labels, top_solved, box_out, scaled_out, near, done):
    right = split(top_coef[...].reshape(CLASSES, RANK))
    sign = signs(labels[...])
    half = LEAF // 2
    copies = []
    for part in range(2):
        rows = slice(part * half, (part + 1) * half)
        solved = inner[rows] - passes(split(top_solved[rows]), right, 1)
        moved = scaled[rows] + sign[rows] * solved
        box = jnp.clip(moved, 0.0, 1.0)
        near[0, rows] = box
        near[1, rows] = moved - box
        for i, out in enumerate((box_out, scaled_out)):
            copy = pltpu.make_async_copy(near.at[i, rows], out.at[rows], done.at[2 * part + i])
            copy.start()
            copies.append(copy)
    for copy in copies:
        copy.wait()


def call(kernel, outs, args, scratch=(), flops=0):
    shapes = [jax.ShapeDtypeStruct(shape, jnp.float32) for shape in outs]
    moved = sum(4 * a.size for a in args) + sum(4 * s.size for s in shapes)
    return pl.pallas_call(
        kernel,
        out_shape=shapes,
        in_specs=[pl.BlockSpec(memory_space=pltpu.VMEM)] * len(args),
        out_specs=[pl.BlockSpec(memory_space=pltpu.VMEM)] * len(outs),
        scratch_shapes=[pltpu.VMEM(shape, jnp.float32) for shape in scratch],
        compiler_params=pltpu.CompilerParams(vmem_limit_bytes=16 * 1024 * 1024),
        cost_estimate=pl.CostEstimate(flops=flops, bytes_accessed=moved, transcendentals=0),
    )(*args)


STACK = (4 * RANK, CLASSES)
WIDE = (LEAF, CLASSES)
TILES = (16, 16, RANK)
COEFFS = (RANK, CLASSES)
UNIT = 6 * RANK * RANK * RANK


def exchange(tiles, axis):
    return lax.all_to_all(tiles, axis, 0, 0, tiled=True)


def across_square(pieces):
    return [pieces[0]] + [lax.ppermute(pieces[q], BOTH, square_pairs(q)) for q in range(1, 4)]


def relayed(coeffs):
    before = lax.ppermute(coeffs, BOTH, mirrored_pairs(1))
    after = lax.ppermute(coeffs, BOTH, mirrored_pairs(-1))
    opposite = lax.ppermute(before, BOTH, mirrored_pairs(1))
    return [coeffs, before, after, opposite]


def top_solve(shares, top_capacitance):
    (coefs,) = call(
        top_kernel, [TILES], [exchange(shares, "grp"), top_capacitance], flops=16 * UNIT
    )
    return exchange(coefs, "leaf")


def shards(
    labels,
    leaf_inverse,
    leaf_basis,
    leaf_solved,
    group_capacitance,
    top_basis,
    top_solved,
    top_capacitance,
):
    labels = labels.reshape(1, LEAF)
    pieces = pl.pallas_call(
        cut_kernel,
        out_shape=[jax.ShapeDtypeStruct((RANK, 4 * RANK), jnp.float32)] * 4,
        in_specs=[pl.BlockSpec(memory_space=pl.ANY)],
        out_specs=[pl.BlockSpec(memory_space=pl.ANY)] * 4,
        scratch_shapes=[pltpu.SemaphoreType.DMA((16,))],
        compiler_params=pltpu.CompilerParams(vmem_limit_bytes=16 * 1024 * 1024),
    )(group_capacitance)
    blocks = across_square(pieces)
    local, coeffs = pl.pallas_call(
        first_kernel,
        out_shape=[
            jax.ShapeDtypeStruct(WIDE, jnp.float32),
            jax.ShapeDtypeStruct(COEFFS, jnp.float32),
        ],
        in_specs=[pl.BlockSpec(memory_space=pl.ANY)] * 3,
        out_specs=[pl.BlockSpec(memory_space=pl.ANY)] * 2,
        scratch_shapes=[
            pltpu.VMEM(labels.shape, labels.dtype),
            pltpu.VMEM(leaf_inverse.shape, jnp.float32),
            pltpu.VMEM(leaf_basis.shape, jnp.float32),
            pltpu.VMEM(WIDE, jnp.float32),
            pltpu.VMEM(COEFFS, jnp.float32),
            pltpu.SemaphoreType.DMA((8,)),
        ],
        compiler_params=pltpu.CompilerParams(vmem_limit_bytes=62900000),
    )(labels, leaf_inverse, leaf_basis)
    lift, folded = call(
        lift_kernel,
        [(RANK, RANK), (RANK // 2, CLASSES)],
        [leaf_solved, top_basis],
        flops=4 * UNIT,
    )
    (projection,) = call(project_kernel, [COEFFS], [local, top_basis], flops=8 * UNIT)
    (reach,) = call(
        reach_kernel,
        [(2 * RANK, LEAF)],
        [leaf_inverse, leaf_basis, top_basis],
        flops=32 * UNIT,
    )
    sent = across_square(
        call(
            group_kernel,
            [(RANK + RANK // 2, CLASSES)] * 4,
            [folded, *blocks, *relayed(coeffs)],
            scratch=[STACK],
            flops=32 * UNIT,
        )
    )
    inner, tiles = call(
        inner_kernel,
        [WIDE, TILES],
        [local, leaf_solved, lift, projection, reach, *sent],
        flops=10 * UNIT,
    )
    (shares,) = call(sum_kernel, [TILES], [exchange(tiles, "leaf")])
    top_coef = top_solve(shares, top_capacitance)

    local, scaled, coeffs, projection = call(
        next_kernel,
        [WIDE, WIDE, COEFFS, COEFFS],
        [inner, top_coef, labels, top_solved, leaf_inverse, reach],
        flops=56 * UNIT,
    )
    (block_lift,) = call(
        block_lift_kernel, [(RANK, 4 * RANK)], [*blocks, *sent], flops=16 * UNIT
    )
    *partials, tiles = call(
        later_group_kernel,
        [COEFFS] * 4 + [TILES],
        [projection, block_lift, *blocks, *relayed(coeffs)],
        scratch=[STACK],
        flops=40 * UNIT,
    )
    shares, inner = call(
        sum_inner_kernel,
        [TILES, WIDE],
        [exchange(tiles, "leaf"), local, leaf_solved, *across_square(partials)],
        flops=8 * UNIT,
    )
    top_coef = top_solve(shares, top_capacitance)
    return tuple(
        pl.pallas_call(
            last_kernel,
            out_shape=[jax.ShapeDtypeStruct(WIDE, jnp.float32)] * 2,
            in_specs=[pl.BlockSpec(memory_space=pltpu.VMEM)] * 5,
            out_specs=[pl.BlockSpec(memory_space=pl.ANY)] * 2,
            scratch_shapes=[
                pltpu.VMEM((2, *WIDE), jnp.float32),
                pltpu.SemaphoreType.DMA((4,)),
            ],
            compiler_params=pltpu.CompilerParams(vmem_limit_bytes=16 * 1024 * 1024),
        )(inner, top_coef, scaled, labels, top_solved)
    )


def solution(mesh):
    rows = P(BOTH, None)
    return jax.shard_map(
        shards,
        mesh=mesh,
        in_specs=(P(BOTH), rows, rows, rows, rows, rows, rows, P("grp", None)),
        out_specs=(rows, rows),
        check_vma=False,
    )
```

```python
import functools

import jax
import jax.numpy as jnp
from jax import lax
from jax.experimental import pallas as pl
from jax.experimental.pallas import tpu as pltpu
from jax.sharding import PartitionSpec as P

CLASSES = 256
RANK = 128
LEAF = 512
BOTH = ("grp", "leaf")


def partner(core, z):
    return (((z + core) ^ 1) - core) % 8


def devices():
    return [(g, i // 8, i % 8) for g in range(16) for i in range(16)]


def index(g, x, z):
    return g * 16 + x * 8 + z


def square_pairs(q):
    pairs = []
    for g, x, z in devices():
        other = index(g, x ^ (q // 2), partner(g % 2, z) if q % 2 else z)
        pairs.append((index(g, x, z), other))
    return pairs


def mirrored_pairs(k):
    sign = (1, -1)
    return [
        (index(g, x, z), index(g, x, (z + 2 * k * sign[g % 2]) % 8)) for g, x, z in devices()
    ]


def split(value):
    high = value.astype(jnp.bfloat16)
    return high, (value - high.astype(jnp.float32)).astype(jnp.bfloat16)


def passes(left, right, right_dim=0):
    def one(a, b):
        return lax.dot_general(
            a, b, (((1,), (right_dim,)), ((), ())), preferred_element_type=jnp.float32
        )

    total = one(left[1], right[0])
    if right[1] is not None:
        total = total + one(left[0], right[1])
    return total + one(left[0], right[0])


def times(left, right, right_dim=0):
    return passes(split(left), split(right), right_dim)


def signs(labels):
    spread = jnp.broadcast_to(labels.astype(jnp.float32), (RANK, LEAF)).T
    lane = lax.broadcasted_iota(jnp.int32, (LEAF, RANK), 1).astype(jnp.float32)
    halves = [jnp.where(spread == lane + RANK * h, 1.0, -1.0) for h in range(2)]
    return jnp.concatenate(halves, axis=1).astype(jnp.float32)


def cut_kernel(capacitance, *refs):
    pieces, done = refs[:4], refs[4]
    leaf = lax.axis_index("leaf")
    x, z = leaf // 8, leaf % 8
    copies = []
    for q in (3, 2, 1, 0):
        first = ((x + q // 2) % 2) * 8 + (z + q) % 2
        for j in range(4):
            start = pl.multiple_of((first + 2 * j) * RANK, RANK)
            copies.append(
                pltpu.make_async_copy(
                    capacitance.at[:, pl.ds(start, RANK)],
                    pieces[q].at[:, j * RANK : (j + 1) * RANK],
                    done.at[4 * q + j],
                )
            )
            copies[-1].start()
    for copy in copies:
        copy.wait()


def first_kernel(labels, inverse, basis, *refs):
    local_out, coeffs_out, near_labels, near, near_basis, local, coeffs, done = refs
    quarter = LEAF // 4
    parts = [slice(k * quarter, (k + 1) * quarter) for k in range(4)]
    copies = [pltpu.make_async_copy(labels, near_labels, done.at[0])]
    for k, rows in enumerate(parts):
        copies.append(pltpu.make_async_copy(inverse.at[rows], near.at[rows], done.at[k + 1]))
    copies.append(pltpu.make_async_copy(basis, near_basis, done.at[5]))
    for copy in copies:
        copy.start()
    copies[0].wait()
    sign = (signs(near_labels[...]).astype(jnp.bfloat16), None)
    for k, rows in enumerate(parts):
        copies[k + 1].wait()
        local[rows] = passes(split(near[rows]), sign)
    leaving = pltpu.make_async_copy(local, local_out, done.at[6])
    leaving.start()
    copies[5].wait()
    coeffs[...] = times(near_basis[...].T, local[...])
    last = pltpu.make_async_copy(coeffs, coeffs_out, done.at[7])
    last.start()
    leaving.wait()
    last.wait()


def lift_kernel(solved, top, lift, folded):
    found = times(top[...].T, solved[...])
    lift[...] = found
    folded[...] = jnp.concatenate([found[: RANK // 2], found[RANK // 2 :]], axis=1)


def project_kernel(local, top, projection):
    projection[...] = times(top[...].T, local[...])


def reach_kernel(inverse, basis, top, reach):
    both = jnp.concatenate([basis[...].T, top[...].T], axis=0)
    reach[...] = times(both, inverse[...])


def block_lift_kernel(*refs):
    blocks, sent, out = refs[:4], refs[4:8], refs[8]
    lifts = []
    for q in range(4):
        lift = sent[q][RANK:, :]
        lifts.append(jnp.concatenate([lift[:, :RANK], lift[:, RANK:]], axis=0))
    block = jnp.concatenate([part[...] for part in blocks], axis=0)
    out[...] = times(jnp.concatenate(lifts, axis=1), block)


def row_of(k):
    sign = 1 - 2 * (lax.axis_index("grp") % 2)
    step = (lax.axis_index("leaf") % 8) // 2
    return pl.ds(pl.multiple_of(((step + k * sign + 4) % 4) * RANK, RANK), RANK)


def group_kernel(lift, *refs):
    blocks, pieces, stacked = refs[:4], refs[4:8], refs[12]
    for piece, k in zip(pieces, (0, -1, 1, 2)):
        stacked[row_of(k), :] = piece[...]
    block = jnp.concatenate([part[...] for part in blocks], axis=0)
    rows = passes(split(block), split(stacked[...]))
    for q in range(4):
        refs[8 + q][:RANK, :] = rows[q * RANK : (q + 1) * RANK]
        refs[8 + q][RANK:, :] = lift[...]


def inner_kernel(local, solved, lift, projection, reach, *refs):
    parts, inner, tiles = refs[:4], refs[4], refs[5]
    coef = (parts[0][:RANK] + parts[1][:RANK]) + (parts[2][:RANK] + parts[3][:RANK])
    both = times(jnp.concatenate([solved[...], lift[...]], axis=0), coef)
    inner[...] = local[...] - both[:LEAF]
    tiles[...] = (projection[...] - both[LEAF:]).T.reshape(16, 16, RANK)


def columns_of(blocks, k):
    return jnp.concatenate([part[:, row_of(k)] for part in blocks], axis=0)


def near_kernel(*refs):
    blocks, pieces, out = refs[:-4], refs[-4:-1], refs[-1]
    left = jnp.concatenate([columns_of(blocks, k) for k in (0, -1, 1)], axis=1)
    right = jnp.concatenate([piece[...] for piece in pieces], axis=0)
    out[...] = times(left, right)


def later_group_kernel(projection, near, far, *refs):
    blocks, partials, tiles = refs[:5], refs[5:9], refs[9]
    rows = near[...] + times(columns_of(blocks, 2), far[...])
    for q in range(4):
        partials[q][...] = rows[q * RANK : (q + 1) * RANK]
    tiles[...] = (projection[...] - rows[4 * RANK :]).T.reshape(16, 16, RANK)


def sum_inner_kernel(tiles, local, solved, *refs):
    parts, out, inner = refs[:4], refs[4], refs[5]
    out[...] = jnp.broadcast_to(jnp.sum(tiles[...], axis=0)[None], (16, 16, RANK))
    coef = (parts[0][...] + parts[1][...]) + (parts[2][...] + parts[3][...])
    inner[...] = local[...] - times(solved[...], coef)


def sum_kernel(tiles, out):
    out[...] = jnp.broadcast_to(jnp.sum(tiles[...], axis=0)[None], (16, 16, RANK))


def top_kernel(gathered, capacitance, out):
    wide = jnp.concatenate([gathered[g] for g in range(16)], axis=1)
    share = times(wide, capacitance[...], 1)
    out[...] = jnp.broadcast_to(share[None], (16, 16, RANK))


def solved_of(inner, top_solved, top_coef):
    return inner[...] - times(top_solved[...], top_coef[...].reshape(CLASSES, RANK), 1)


def next_kernel(
    inner, top_coef, labels, top_solved, inverse, reach, local, scaled, coeffs, projection
):
    sign = signs(labels[...])
    moved = sign * solved_of(inner, top_solved, top_coef)
    box = jnp.clip(moved, 0.0, 1.0)
    rest = moved - box
    scaled[...] = rest
    both = jnp.concatenate([inverse[...], reach[...]], axis=0)
    found = times(both, sign * (1.0 + (box - rest)))
    local[...] = found[:LEAF]
    coeffs[...] = found[LEAF : LEAF + RANK]
    projection[...] = found[LEAF + RANK :]


def last_kernel(inner, top_coef, scaled, labels, top_solved, box_out, scaled_out, near, done):
    right = split(top_coef[...].reshape(CLASSES, RANK))
    sign = signs(labels[...])
    half = LEAF // 2
    copies = []
    for part in range(2):
        rows = slice(part * half, (part + 1) * half)
        solved = inner[rows] - passes(split(top_solved[rows]), right, 1)
        moved = scaled[rows] + sign[rows] * solved
        box = jnp.clip(moved, 0.0, 1.0)
        near[0, rows] = box
        near[1, rows] = moved - box
        for i, out in enumerate((box_out, scaled_out)):
            copy = pltpu.make_async_copy(near.at[i, rows], out.at[rows], done.at[2 * part + i])
            copy.start()
            copies.append(copy)
    for copy in copies:
        copy.wait()


def call(kernel, outs, args, scratch=(), flops=0):
    shapes = [jax.ShapeDtypeStruct(shape, jnp.float32) for shape in outs]
    moved = sum(4 * a.size for a in args) + sum(4 * s.size for s in shapes)
    return pl.pallas_call(
        kernel,
        out_shape=shapes,
        in_specs=[pl.BlockSpec(memory_space=pltpu.VMEM)] * len(args),
        out_specs=[pl.BlockSpec(memory_space=pltpu.VMEM)] * len(outs),
        scratch_shapes=[pltpu.VMEM(shape, jnp.float32) for shape in scratch],
        compiler_params=pltpu.CompilerParams(vmem_limit_bytes=16 * 1024 * 1024),
        cost_estimate=pl.CostEstimate(flops=flops, bytes_accessed=moved, transcendentals=0),
    )(*args)


STACK = (4 * RANK, CLASSES)
WIDE = (LEAF, CLASSES)
TILES = (16, 16, RANK)
COEFFS = (RANK, CLASSES)
UNIT = 6 * RANK * RANK * RANK


def exchange(tiles, axis):
    return lax.all_to_all(tiles, axis, 0, 0, tiled=True)


def across_square(pieces):
    return [pieces[0]] + [lax.ppermute(pieces[q], BOTH, square_pairs(q)) for q in range(1, 4)]


def diagonal_first(parts):
    return [parts[0], parts[3], parts[2], parts[1]]


def relayed(coeffs):
    before = lax.ppermute(coeffs, BOTH, mirrored_pairs(1))
    after = lax.ppermute(coeffs, BOTH, mirrored_pairs(-1))
    opposite = lax.ppermute(before, BOTH, mirrored_pairs(1))
    return [coeffs, before, after, opposite]


def top_solve(shares, top_capacitance):
    (coefs,) = call(
        top_kernel, [TILES], [exchange(shares, "grp"), top_capacitance], flops=16 * UNIT
    )
    return exchange(coefs, "leaf")


def shards(
    labels,
    leaf_inverse,
    leaf_basis,
    leaf_solved,
    group_capacitance,
    top_basis,
    top_solved,
    top_capacitance,
):
    labels = labels.reshape(1, LEAF)
    pieces = pl.pallas_call(
        cut_kernel,
        out_shape=[jax.ShapeDtypeStruct((RANK, 4 * RANK), jnp.float32)] * 4,
        in_specs=[pl.BlockSpec(memory_space=pl.ANY)],
        out_specs=[pl.BlockSpec(memory_space=pl.ANY)] * 4,
        scratch_shapes=[pltpu.SemaphoreType.DMA((16,))],
        compiler_params=pltpu.CompilerParams(vmem_limit_bytes=16 * 1024 * 1024),
    )(group_capacitance)
    blocks = across_square(pieces)
    local, coeffs = pl.pallas_call(
        first_kernel,
        out_shape=[
            jax.ShapeDtypeStruct(WIDE, jnp.float32),
            jax.ShapeDtypeStruct(COEFFS, jnp.float32),
        ],
        in_specs=[pl.BlockSpec(memory_space=pl.ANY)] * 3,
        out_specs=[pl.BlockSpec(memory_space=pl.ANY)] * 2,
        scratch_shapes=[
            pltpu.VMEM(labels.shape, labels.dtype),
            pltpu.VMEM(leaf_inverse.shape, jnp.float32),
            pltpu.VMEM(leaf_basis.shape, jnp.float32),
            pltpu.VMEM(WIDE, jnp.float32),
            pltpu.VMEM(COEFFS, jnp.float32),
            pltpu.SemaphoreType.DMA((8,)),
        ],
        compiler_params=pltpu.CompilerParams(vmem_limit_bytes=62900000),
    )(labels, leaf_inverse, leaf_basis)
    lift, folded = call(
        lift_kernel,
        [(RANK, RANK), (RANK // 2, CLASSES)],
        [leaf_solved, top_basis],
        flops=4 * UNIT,
    )
    (projection,) = call(project_kernel, [COEFFS], [local, top_basis], flops=8 * UNIT)
    (reach,) = call(
        reach_kernel,
        [(2 * RANK, LEAF)],
        [leaf_inverse, leaf_basis, top_basis],
        flops=32 * UNIT,
    )
    sent = across_square(
        call(
            group_kernel,
            [(RANK + RANK // 2, CLASSES)] * 4,
            [folded, *blocks, *relayed(coeffs)],
            scratch=[STACK],
            flops=32 * UNIT,
        )
    )
    inner, tiles = call(
        inner_kernel,
        [WIDE, TILES],
        [local, leaf_solved, lift, projection, reach, *diagonal_first(sent)],
        flops=10 * UNIT,
    )
    (shares,) = call(sum_kernel, [TILES], [exchange(tiles, "leaf")])
    top_coef = top_solve(shares, top_capacitance)

    local, scaled, coeffs, projection = call(
        next_kernel,
        [WIDE, WIDE, COEFFS, COEFFS],
        [inner, top_coef, labels, top_solved, leaf_inverse, reach],
        flops=56 * UNIT,
    )
    (block_lift,) = call(
        block_lift_kernel, [(RANK, 4 * RANK)], [*blocks, *sent], flops=16 * UNIT
    )
    blocks = [*blocks, block_lift]
    *pieces, far = relayed(coeffs)
    (near,) = call(
        near_kernel, [(5 * RANK, CLASSES)], [*blocks, *pieces], flops=30 * UNIT
    )
    *partials, tiles = call(
        later_group_kernel,
        [COEFFS] * 4 + [TILES],
        [projection, near, far, *blocks],
        flops=10 * UNIT,
    )
    shares, inner = call(
        sum_inner_kernel,
        [TILES, WIDE],
        [
            exchange(tiles, "leaf"),
            local,
            leaf_solved,
            *diagonal_first(across_square(partials)),
        ],
        flops=8 * UNIT,
    )
    top_coef = top_solve(shares, top_capacitance)
    return tuple(
        pl.pallas_call(
            last_kernel,
            out_shape=[jax.ShapeDtypeStruct(WIDE, jnp.float32)] * 2,
            in_specs=[pl.BlockSpec(memory_space=pltpu.VMEM)] * 5,
            out_specs=[pl.BlockSpec(memory_space=pl.ANY)] * 2,
            scratch_shapes=[
                pltpu.VMEM((2, *WIDE), jnp.float32),
                pltpu.SemaphoreType.DMA((4,)),
            ],
            compiler_params=pltpu.CompilerParams(vmem_limit_bytes=16 * 1024 * 1024),
        )(inner, top_coef, scaled, labels, top_solved)
    )


def solution(mesh):
    rows = P(BOTH, None)
    return jax.shard_map(
        shards,
        mesh=mesh,
        in_specs=(P(BOTH), rows, rows, rows, rows, rows, rows, P("grp", None)),
        out_specs=(rows, rows),
        check_vma=False,
    )
```
